256 devices in a mesh: expert: 32 (over y, z), cuts: 8 (over x, core).
Axes of the slice: x: 4, y: 4, z: 8, core: 2. Of those that a mesh axis runs over, the one named last changes fastest.
Arguments:
- tokens: bfloat16 [8192, 3072], P('expert', 'cuts'), may hold values from -6 to 6
- out_grad: bfloat16 [8192, 3072], P('expert', 'cuts'), may hold values from -3 to 3
- gate_logit: float32 [8192], P('expert'), may hold values from -2 to 2
- expert_ids: int32 [8192, 1], P('expert'), may hold values from 0 to 31; in each aligned block of 256 rows (0 to 255, 256 to 511, ...) at most 16 rows name the same one
- w_gate: bfloat16 [32, 3072, 4096], P('expert', None, 'cuts'), may hold values from -0.109375 to 0.109375
- w_up: bfloat16 [32, 3072, 4096], P('expert', None, 'cuts'), may hold values from -0.109375 to 0.109375
- w_down: bfloat16 [32, 4096, 3072], P('expert', 'cuts'), may hold values from -0.09375 to 0.09375
Outputs:
- input_grad: bfloat16 [8192, 3072], P('expert', 'cuts')
- logit_grad: float32 [8192], P('expert')
- down_stats: float32 [32, 3, 1024, 1024], P('expert', None, 'cuts')
The draws below stay inside these ranges and needn't reach their ends.
Inputs may be any that keep to these rules, and one draw needn't show every extreme that they name: `expert_ids`: in the rows of one device (aligned blocks of 256 rows) no expert is named by more than 16 rows, and in every draw some expert is named by exactly 16 rows of some device.
All inputs are finite; a program needn't handle non-finite values.
Results may differ from the reference program's by a relative error of at most 0.019.
Values may be sent and summed in bfloat16 or wider, within the bound.
No kernel may reach another device: no remote copies, remote signals or barrier semaphores. Data moves between devices by JAX's collectives and lax.ppermute only.
A program may use at most 128 MiB of HBM per device.

```python
import math
import jax
import jax.numpy as jnp
import numpy as np
from jax import lax

D = 3072
FF = 4096
BLOCK = 1024
TOK_DEV = 256
TOKENS = 8192
EXPERTS = 32
CAP = 16
BLOCKS = 3
N_CUTS = 8


def block_scale(rng, extent, split, low, high):
    def one(position, shards_of):
        draws = jax.random.uniform(jax.random.fold_in(jax.random.fold_in(rng, 6), position), (shards_of,), jnp.float32, low / len(split), high / len(split))
        return jnp.repeat(jnp.exp(draws), extent[position] // shards_of).reshape((-1,) + (1,) * (len(extent) - position - 1))

    factor_of = one(*split[0])
    for cut in split[1:]:
        factor_of = factor_of * one(*cut)
    return factor_of


def deal_out(own_key, own, number, rows, amount, top, limit, slope):
    sequence = jax.random.permutation(own_key, amount)
    crowded, usual = load_shares(amount, rows * top, limit, slope, True), load_shares(amount, rows * top, limit, slope, False)
    places = jnp.arange(amount)

    def named(lengths, offset_by):
        used = int((lengths > 0).sum())
        fixed = max(1, used // 4)
        shifted = fixed + (places - fixed + offset_by * (used - fixed)) % max(1, amount - fixed)
        return jnp.zeros((amount,), jnp.int32).at[sequence[jnp.where(places < fixed, places, shifted)]].set(jnp.asarray(lengths, jnp.int32))

    lengths = jnp.where(number % 4 == 0, named(crowded, number // 4), named(usual, number - number // 4 - 1))
    mixed = jax.random.permutation(jax.random.fold_in(own, 3), amount)
    source_of, receiver = mixed[0:amount // 2 * 2:2], mixed[1:amount // 2 * 2:2]
    margin = jnp.minimum(lengths[source_of] - 1, limit - lengths[receiver]) // 2
    margin = jnp.where((source_of == sequence[0]) | (receiver == sequence[0]) | (lengths[receiver] == 0), 0, jnp.maximum(margin, 0))
    shifted = jax.random.randint(jax.random.fold_in(own, 4), (amount // 2,), 0, 1 << 20) % (margin + 1)
    lengths = lengths.at[source_of].add(-shifted).at[receiver].add(shifted)
    labels = jnp.searchsorted(jnp.cumsum(lengths), jnp.arange(rows * top), side="right").astype(jnp.int32)
    table = labels.reshape(top, rows).T
    table = table[jax.random.permutation(jax.random.fold_in(own, 1), rows)]
    offset_by = jax.random.randint(jax.random.fold_in(own, 2), (rows, 1), 0, top)
    return jnp.take_along_axis(table, (jnp.arange(top)[None, :] + offset_by) % top, axis=1)


def load_shares(amount, total, bound, skew, full):
    weights = [(1 << 20) // math.isqrt(standing ** skew) + 1 for standing in range(1, amount + 1)]
    largest = bound if full else min(bound, max(-(-total // amount), total * weights[0] // sum(weights)))
    least = 1 if total - largest >= amount - 1 else 0
    holding, spare = [largest] + [least] * (amount - 1), total - largest - least * (amount - 1)
    while spare > 0:
        candidates = [i for i in range(1, amount) if holding[i] < largest] or [i for i in range(1, amount) if holding[i] < bound]
        whole, remaining = sum([weights[i] for i in candidates]), spare
        for i in candidates:
            more = min(bound - holding[i], max(1, remaining * weights[i] // whole), spare)
            holding[i] = holding[i] + more
            spare = spare - more
    return np.array(holding)


def scatter_about(own_key, extent, scale, bound, shards=(), held_as=jnp.bfloat16):
    entries = scale * jax.random.normal(own_key, extent, jnp.float32)
    if shards:
        entries = entries * block_scale(own_key, extent, shards, -0.22, 0.18)
    return jnp.clip(entries, -bound, bound).astype(held_as)


def setup_inputs(seed: int = 0) -> dict:
    key_of = jax.random.split(jax.random.key(seed), 8)
    tokens = scatter_about(key_of[0], (TOKENS, D), 1.0, 6.0, ((0, 32), (1, 8)))
    out_grad = scatter_about(key_of[1], (TOKENS, D), 0.5, 3.0, ((0, 32), (1, 8)))
    gate_logit = jnp.clip(jax.random.uniform(key_of[2], (TOKENS,), jnp.float32, -2.0, 2.0) * block_scale(key_of[2], (TOKENS,), ((0, 32),), -0.4, 0.0), -2.0, 2.0)
    expert_ids_keys = jax.random.split(jax.random.fold_in(key_of[3], 1), TOKENS // TOK_DEV)
    expert_ids_turns = jax.random.permutation(jax.random.fold_in(key_of[3], 3), TOKENS // TOK_DEV)
    expert_ids = jax.vmap(lambda own, number: deal_out(jax.random.fold_in(key_of[3], 2), own, number, TOK_DEV, EXPERTS, 1, CAP, 2))(expert_ids_keys, expert_ids_turns).reshape((TOKENS, 1))
    w_gate = scatter_about(key_of[4], (EXPERTS, D, FF), D ** -0.5, 0.109375, ((0, 32), (2, 8)))
    w_up = scatter_about(key_of[5], (EXPERTS, D, FF), D ** -0.5, 0.109375, ((0, 32), (2, 8)))
    w_down = scatter_about(key_of[6], (EXPERTS, FF, D), FF ** -0.5, 0.09375, ((0, 32), (1, 8)))
    return {"tokens": tokens, "out_grad": out_grad, "gate_logit": gate_logit, "expert_ids": expert_ids, "w_gate": w_gate, "w_up": w_up, "w_down": w_down}


def reference(tokens, out_grad, gate_logit, expert_ids, w_gate, w_up, w_down):
    gate_score = jax.nn.sigmoid(gate_logit.astype(jnp.float32))
    weighted = (gate_score[:, None] * out_grad.astype(jnp.float32)).astype(jnp.bfloat16)
    routed = expert_ids[:, 0].astype(jnp.int32)
    experts = w_gate.shape[0]
    slots = 2 * TOK_DEV
    onehot = (routed[:, None] == jnp.arange(experts, dtype=jnp.int32)[None, :]).astype(jnp.int32)
    arrival = jnp.sum((jnp.cumsum(onehot, axis=0) - 1) * onehot, axis=1).astype(jnp.int32)
    everyone = jnp.arange(TOKENS, dtype=jnp.int32)
    table = jnp.zeros((experts, slots), jnp.int32).at[routed, arrival].set(everyone)
    filled = jnp.zeros((experts, slots), jnp.int32).at[routed, arrival].set(1)
    width = FF // N_CUTS

    def one_expert(expert):
        members = table[expert]
        present = filled[expert][:, None] > 0
        routed_tok = jnp.where(present, tokens[members], jnp.zeros((), jnp.bfloat16))
        routed_wt = jnp.where(present, weighted[members], jnp.zeros((), jnp.bfloat16))
        gate_mat = w_gate[expert]
        up_mat = w_up[expert]
        down_mat = w_down[expert]
        gate_pre = jnp.dot(routed_tok, gate_mat, preferred_element_type=jnp.float32)
        up_pre = jnp.dot(routed_tok, up_mat, preferred_element_type=jnp.float32)
        gate_sig = jax.nn.sigmoid(gate_pre)
        gate_act = gate_pre * gate_sig
        hidden = (gate_act * up_pre).astype(jnp.bfloat16)
        hidden_grad = jnp.dot(routed_wt, down_mat.T, preferred_element_type=jnp.float32)
        silu_slope = gate_sig * (1.0 + gate_pre * (1.0 - gate_sig))
        gate_grad = (hidden_grad * up_pre * silu_slope).astype(jnp.bfloat16)
        up_grad = (hidden_grad * gate_act).astype(jnp.bfloat16)
        rows = gate_grad.shape[0]
        parts = jnp.einsum("rkf,dkf->krd", gate_grad.reshape(rows, N_CUTS, width).astype(jnp.float32),
                           gate_mat.reshape(D, N_CUTS, width).astype(jnp.float32))
        parts = parts + jnp.einsum("rkf,dkf->krd", up_grad.reshape(rows, N_CUTS, width).astype(jnp.float32),
                                   up_mat.reshape(D, N_CUTS, width).astype(jnp.float32))
        parts = parts.astype(jnp.bfloat16).astype(jnp.float32)
        input_rows = jnp.sum(parts, axis=0).astype(jnp.bfloat16)
        gate_dot = jnp.sum(hidden.astype(jnp.float32) * hidden_grad, axis=1).astype(jnp.bfloat16)
        grad_down = lax.dot_general(hidden, routed_wt, (((0,), (0,)), ((), ())),
                                    preferred_element_type=jnp.float32).astype(jnp.bfloat16)
        blocked = grad_down.astype(jnp.float32).reshape(FF, BLOCKS, BLOCK)
        stats = jnp.einsum("fkb,fkc->kbc", blocked, blocked, precision=lax.Precision.HIGHEST) / FF
        return input_rows, gate_dot, stats

    input_all, dot_all, down_stats = lax.map(one_expert, jnp.arange(experts, dtype=jnp.int32))
    input_grad = input_all[routed, arrival]
    gate_dot = dot_all[routed, arrival].astype(jnp.float32)
    logit_grad = (1.0 - gate_score) * gate_dot
    return input_grad, logit_grad, down_stats
```

```python
import functools

import jax
import jax.numpy as jnp
from jax import lax
from jax.experimental import pallas as pl
from jax.experimental.pallas import tpu as pltpu
from jax.sharding import PartitionSpec as P

FF = 4096
BLOCK = 1024
F32 = jnp.float32
BF16 = jnp.bfloat16
VMEM = pltpu.VMEM
LAST = (((1,), (1,)), ((), ()))
FIRST = (((0,), (0,)), ((), ()))


def dot(a, b, dims=(((1,), (0,)), ((), ()))):
    return lax.dot_general(a, b, dims, preferred_element_type=F32)


def iota(shape, dim):
    return lax.broadcasted_iota(jnp.int32, shape, dim)


def whole():
    return pl.BlockSpec(memory_space=VMEM)


def call(body, out, inputs, flops=0, name=None, scratch=(), scalars=1, limit=48):
    moved = sum(x.size * x.dtype.itemsize for x in inputs) + sum(
        o.size * o.dtype.itemsize for o in out
    )
    specs = [pl.BlockSpec(memory_space=pltpu.SMEM)] * scalars
    specs += [whole()] * (len(inputs) - scalars)
    return pl.pallas_call(
        body,
        out_shape=out,
        in_specs=specs,
        out_specs=[whole()] * len(out),
        scratch_shapes=list(scratch),
        compiler_params=pltpu.CompilerParams(vmem_limit_bytes=limit << 20),
        cost_estimate=pl.CostEstimate(flops=flops, bytes_accessed=moved, transcendentals=0),
        name=name,
    )(*inputs)


def column(row):
    return jnp.transpose(jnp.broadcast_to(row, (8, row.shape[1])))[:, :1]


def pack_kernel(capacity, ids_ref, logit_ref, tok_ref, grad_ref, tok_out, wt_out, slot_out):
    ids = ids_ref[...]
    rows = ids.shape[1]
    total = tok_out.shape[0]
    mine = ids == iota((total // capacity, rows), 0)
    earlier = (iota((rows, rows), 0) < iota((rows, rows), 1)).astype(F32).astype(BF16)
    before = dot(mine.astype(F32).astype(BF16), earlier)
    arrival = jnp.sum(jnp.where(mine, before, 0.0), axis=0, keepdims=True)
    slot = ids * capacity + arrival.astype(jnp.int32)
    slot_out[...] = jnp.broadcast_to(slot, slot_out.shape)
    place = (slot == iota((total, rows), 0)).astype(F32).astype(BF16)
    tok_out[...] = dot(place, tok_ref[...]).astype(BF16)
    score = column(jax.nn.sigmoid(logit_ref[...]))
    weighted = (score * grad_ref[...].astype(F32)).astype(BF16)
    wt_out[...] = dot(place, weighted).astype(BF16)


def unpack_kernel(slot_ref, logit_ref, back_ref, grad_out, logit_out):
    total = back_ref.shape[0]
    rows, width = grad_out.shape
    slot = jnp.transpose(slot_ref[...])[:, :1]
    place = (slot == iota((rows, total), 1)).astype(F32).astype(BF16)
    own = dot(place, back_ref[...])
    grad_out[...] = own[:, :width].astype(BF16)
    gate_dot = jnp.transpose(own[:, width:])[:1]
    logit_out[...] = (1.0 - jax.nn.sigmoid(logit_ref[...])) * gate_dot


def block_of(cut, hop, other, chips):
    chip = (cut // 2 + chips - hop) % chips
    core = cut % 2
    return 2 * chip + (1 - core if other else core)


def at(index, size):
    return pl.ds(pl.multiple_of(index * size, size), size)


def gates_kernel(chips, cut_ref, *refs):
    near, far = refs[:chips], refs[chips : 2 * chips]
    gate_ref, up_ref, hid_out, act_out, slope_out, send_out, keep_out, gram = refs[2 * chips :]
    cut = cut_ref[0]
    width = near[0].shape[1]
    for ref, out in ((gate_ref, act_out), (up_ref, slope_out)):
        for k in range(chips):
            rows = jnp.concatenate([near[k][...], far[k][...]], axis=1)
            mat = jnp.concatenate(
                [ref[at(block_of(cut, k, o, chips), width), :] for o in (False, True)], axis=0
            )
            if k == 0:
                out[...] = dot(rows, mat)
            else:
                out[...] += dot(rows, mat)
    gate_pre = act_out[...]
    up_pre = slope_out[...]
    sig = jax.nn.sigmoid(gate_pre)
    act = gate_pre * sig
    hidden = (act * up_pre).astype(BF16)
    act_out[...] = act
    slope_out[...] = up_pre * (sig * (1.0 + gate_pre * (1.0 - sig)))
    hid_out[...] = hidden
    gram[...] = dot(hidden, hidden, LAST)
    half = send_out.shape[0]
    keep_out[...] = gram[at(cut % 2, half), :].astype(BF16)
    send_out[...] = gram[at(1 - cut % 2, half), :].astype(BF16)


def hidden_kernel(chips, cut_ref, *refs):
    near, far = refs[:chips], refs[chips : 2 * chips]
    down_ref, hid_ref, act_ref, slope_ref, both_out, dot_out, acc = refs[2 * chips :]
    cut = cut_ref[0]
    width = near[0].shape[1]
    for k in range(chips):
        rows = jnp.concatenate([near[k][...], far[k][...]], axis=1)
        mat = jnp.concatenate(
            [down_ref[:, at(block_of(cut, k, o, chips), width)] for o in (False, True)], axis=1
        )
        if k == 0:
            acc[...] = dot(rows, mat, LAST)
        else:
            acc[...] += dot(rows, mat, LAST)
    grad = acc[...]
    ff = grad.shape[1]
    both_out[:, :ff] = (grad * slope_ref[...]).astype(BF16)
    both_out[:, ff:] = (grad * act_ref[...]).astype(BF16)
    dots = jnp.sum(hid_ref[...].astype(F32) * grad, axis=1, keepdims=True)
    dot_out[...] = jnp.transpose(jnp.broadcast_to(dots, (dots.shape[0], 128)))[:8]


def part_kernel(where_ref, both_ref, gate_own, gate_oth, up_own, up_oth, keep_out, send_out):
    gate = jnp.concatenate([gate_own[...], gate_oth[...]], axis=0)
    up = jnp.concatenate([up_own[...], up_oth[...]], axis=0)
    out = dot(both_ref[...], jnp.concatenate([gate, up], axis=1), LAST).astype(BF16)
    width = keep_out.shape[1]
    keep_out[...] = out[:, :width]
    send_out[...] = out[:, width:]


def part(where, both, gate_mat, up_mat, width):
    rows, ff = both.shape[0], gate_mat.shape[1]
    mats = [pl.BlockSpec((width, ff), lambda i, w, j=j: (w[j], 0)) for j in (0, 1, 0, 1)]
    out = jax.ShapeDtypeStruct((rows, width), BF16)
    full = pl.BlockSpec((rows, width), lambda i, w: (0, 0))
    return pl.pallas_call(
        part_kernel,
        out_shape=[out, out],
        grid_spec=pltpu.PrefetchScalarGridSpec(
            num_scalar_prefetch=1,
            grid=(1,),
            in_specs=[pl.BlockSpec((rows, 2 * ff), lambda i, w: (0, 0))] + mats,
            out_specs=[full, full],
        ),
        compiler_params=pltpu.CompilerParams(vmem_limit_bytes=48 << 20),
        cost_estimate=pl.CostEstimate(
            flops=8 * rows * ff * width, bytes_accessed=6 << 20, transcendentals=0
        ),
        name="input_part",
    )(where, both, gate_mat, gate_mat, up_mat, up_mat)


def final_kernel(chips, *refs):
    sums, dots, out = refs[:chips], refs[chips : 2 * chips], refs[2 * chips]
    total = sums[0][...].astype(F32)
    gate_dot = dots[0][...]
    for k in range(1, chips):
        total = total + sums[k][...].astype(F32)
        gate_dot = gate_dot + dots[k][...]
    width = total.shape[1]
    out[:, :width] = total.astype(BF16)
    lane = jnp.transpose(jnp.broadcast_to(gate_dot[:1], (128, gate_dot.shape[1])))
    out[:, width:] = lane.astype(BF16)


def split_kernel(chips, cut_ref, keep_ref, recv_ref, *refs):
    outs, half = refs[:chips], refs[chips]
    half[...] = keep_ref[...].astype(F32) + recv_ref[...].astype(F32)
    chip = cut_ref[0] // 2
    for k in range(chips):
        outs[k][...] = half[at((chip + k) % chips, outs[k].shape[0]), :].astype(BF16)


def stats_kernel(chips, cut_ref, *refs):
    near, far = refs[:chips], refs[chips : 2 * chips]
    own_k = refs[2 * chips : 3 * chips]
    oth_k, out, rows, gram = refs[3 * chips :]
    cut = cut_ref[0]
    width = near[0].shape[1]
    piece = own_k[0].shape[0]
    for k in range(chips):
        rows[:, at(block_of(cut, k, False, chips), width)] = near[k][...]
        rows[:, at(block_of(cut, k, True, chips), width)] = far[k][...]
        chip = (cut // 2 + chips - k) % chips
        gram[at(cut % 2 * chips + chip, piece), :] = own_k[k][...]
        gram[at((1 - cut % 2) * chips + chip, piece), :] = oth_k[k * piece : (k + 1) * piece, :]
    share = out.shape[1]
    blocks = out.shape[0]
    per = BLOCK // share
    own = jnp.concatenate([rows[:, at(per * j + cut, share)] for j in range(blocks)], axis=1)
    mixed = dot(gram[...], own).astype(BF16)
    for j in range(blocks):
        out[j] = dot(
            mixed[:, j * share : (j + 1) * share], rows[:, j * BLOCK : (j + 1) * BLOCK], FIRST
        ) * (1.0 / FF)


def shards(tokens, out_grad, gate_logit, expert_ids, w_gate, w_up, w_down):
    experts = lax.axis_size("expert")
    cuts = lax.axis_size("cuts")
    chips = cuts // 2
    tok_rows, width = tokens.shape
    capacity = 2 * tok_rows // experts
    total = experts * capacity
    gate_mat, up_mat, down_mat = w_gate[0], w_up[0], w_down[0]
    ff, feats = down_mat.shape
    shape = jax.ShapeDtypeStruct
    cut = lax.axis_index("cuts").astype(jnp.int32)
    where = cut.reshape(1)

    def hop(x, k):
        if k == 0:
            return x
        return lax.ppermute(
            x, "cuts", [(2 * i + c, 2 * ((i + k) % chips) + c) for i in range(chips) for c in (0, 1)]
        )

    def swap(x):
        return lax.ppermute(x, "cuts", [(i, i ^ 1) for i in range(cuts)])

    def exchange(x):
        return lax.all_to_all(x, "expert", split_axis=0, concat_axis=0, tiled=True)

    order = [0, 1, 3, 2]
    ids = expert_ids.reshape(1, tok_rows)
    logit = gate_logit.reshape(1, tok_rows)
    tok_pack, wt_pack, slot = call(
        functools.partial(pack_kernel, capacity),
        [
            shape((total, width), BF16),
            shape((total, width), BF16),
            shape((8, tok_rows), jnp.int32),
        ],
        (ids, logit, tokens, out_grad),
        4 * total * tok_rows * width,
        "pack",
        scalars=0,
    )

    def gathered(packed):
        rows = exchange(packed.reshape(experts, capacity, width)).reshape(total, width)
        near = [hop(rows, k) for k in range(chips)]
        return near, [swap(x) for x in near]

    tok_near, tok_far = gathered(tok_pack)
    wt_near, wt_far = gathered(wt_pack)

    half = total // 2
    hidden, act, slope, gram_send, gram_keep = call(
        functools.partial(gates_kernel, chips),
        [
            shape((total, ff), BF16),
            shape((total, ff), F32),
            shape((total, ff), F32),
            shape((half, total), BF16),
            shape((half, total), BF16),
        ],
        (where, *tok_near, *tok_far, gate_mat, up_mat),
        4 * total * feats * ff + 2 * total * total * ff,
        "gates",
        scratch=[VMEM((total, total), F32)],
    )
    both, dots = call(
        functools.partial(hidden_kernel, chips),
        [shape((total, 2 * ff), BF16), shape((8, total), F32)],
        (where, *wt_near, *wt_far, down_mat, hidden, act, slope),
        2 * total * feats * ff,
        "hidden_grad",
        scratch=[VMEM((total, ff), F32)],
    )

    chip, core = cut // 2, cut % 2
    sums = [None] * chips
    for k in (2, 1, 3, 0):
        base = 2 * ((chip + k) % chips)
        keep, send = part(
            jnp.stack([base + core, base + 1 - core]), both, gate_mat, up_mat, width
        )
        chip_sum = (keep.astype(F32) + swap(send).astype(F32)).astype(BF16)
        sums[k] = hop(chip_sum, k)
    chip_dots = dots + swap(dots)
    all_dots = [hop(chip_dots, k) for k in range(chips)]

    pieces = call(
        functools.partial(split_kernel, chips),
        [shape((half // chips, total), BF16)] * chips,
        (where, gram_keep, swap(gram_send)),
        0,
        "gram_split",
        scratch=[VMEM((half, total), F32)],
    )
    mine = sum(hop(pieces[k], k).astype(F32) for k in range(chips)).astype(BF16)
    gram_own = [hop(mine, k) for k in range(chips)]
    gram_oth = swap(jnp.concatenate(gram_own, axis=0))
    blocks = feats // BLOCK
    (stats,) = call(
        functools.partial(stats_kernel, chips),
        [shape((blocks, BLOCK // cuts, BLOCK), F32)],
        (where, *wt_near, *wt_far, *gram_own, gram_oth),
        4 * total * total * feats // cuts + 2 * total * BLOCK * feats // cuts,
        "stats",
        scratch=[VMEM((total, feats), BF16), VMEM((total, total), BF16)],
    )

    (payload,) = call(
        functools.partial(final_kernel, chips),
        [shape((total, width + 128), BF16)],
        (*sums, *all_dots),
        0,
        "final",
        scalars=0,
    )
    back = exchange(payload.reshape(experts, capacity, width + 128)).reshape(total, width + 128)
    input_grad, logit_grad = call(
        unpack_kernel,
        [shape((tok_rows, width), BF16), shape((1, tok_rows), F32)],
        (slot, logit, back),
        2 * tok_rows * total * (width + 128),
        "unpack",
        scalars=0,
    )
    return input_grad, logit_grad.reshape(tok_rows), stats[None]


def solution(mesh):
    return jax.shard_map(
        shards,
        mesh=mesh,
        in_specs=(
            P("expert", "cuts"),
            P("expert", "cuts"),
            P("expert"),
            P("expert", None),
            P("expert", None, "cuts"),
            P("expert", None, "cuts"),
            P("expert", "cuts", None),
        ),
        out_specs=(P("expert", "cuts"), P("expert"), P("expert", None, "cuts", None)),
        check_vma=False,
    )
```

```python
import functools

import jax
import jax.numpy as jnp
from jax import lax
from jax.experimental import pallas as pl
from jax.experimental.pallas import tpu as pltpu
from jax.sharding import PartitionSpec as P

FF = 4096
BLOCK = 1024
F32 = jnp.float32
BF16 = jnp.bfloat16
VMEM = pltpu.VMEM
LAST = (((1,), (1,)), ((), ()))
FIRST = (((0,), (0,)), ((), ()))


def dot(a, b, dims=(((1,), (0,)), ((), ()))):
    return lax.dot_general(a, b, dims, preferred_element_type=F32)


def iota(shape, dim):
    return lax.broadcasted_iota(jnp.int32, shape, dim)


def whole():
    return pl.BlockSpec(memory_space=VMEM)


def call(body, out, inputs, flops=0, name=None, scratch=(), scalars=1, limit=14, after=(), light=False):
    moved = sum(x.size * x.dtype.itemsize for x in inputs) + sum(
        o.size * o.dtype.itemsize for o in out
    )
    if light:
        flops, moved = 0, 0
    specs = [pl.BlockSpec(memory_space=pltpu.SMEM)] * scalars
    specs += [whole()] * (len(inputs) - scalars)
    specs += [pl.BlockSpec(memory_space=pl.ANY)] * len(after)
    count = len(inputs)

    def kernel(*refs):
        body(*refs[:count], *refs[count + len(after) :])

    return pl.pallas_call(
        kernel,
        out_shape=out,
        in_specs=specs,
        out_specs=[whole()] * len(out),
        scratch_shapes=list(scratch),
        compiler_params=pltpu.CompilerParams(vmem_limit_bytes=limit << 20),
        cost_estimate=pl.CostEstimate(flops=flops, bytes_accessed=moved, transcendentals=0),
        name=name,
    )(*inputs, *after)


def column(row):
    return jnp.transpose(jnp.broadcast_to(row, (8, row.shape[1])))[:, :1]


def pack_kernel(capacity, cut_ref, ids_hbm, logit_hbm, tok_hbm, grad_hbm, out, slot_out, *scratch):
    ids_ref, logit_ref, tok_ref, grad_ref, sems = scratch
    copies = [
        pltpu.make_async_copy(src, dst, sems.at[n])
        for n, (src, dst) in enumerate(
            [
                (ids_hbm, ids_ref),
                (logit_hbm, logit_ref),
                (grad_hbm, grad_ref),
                (tok_hbm, tok_ref),
            ]
        )
    ]
    for copy in copies:
        copy.start()
    copies[0].wait()
    ids = ids_ref[...]
    rows, width = tok_ref.shape
    total = out.shape[0]
    mine = ids == iota((total // capacity, rows), 0)
    earlier = (iota((rows, rows), 0) < iota((rows, rows), 1)).astype(F32).astype(BF16)
    before = dot(mine.astype(F32).astype(BF16), earlier)
    arrival = jnp.sum(jnp.where(mine, before, 0.0), axis=0, keepdims=True)
    slot = ids * capacity + arrival.astype(jnp.int32)
    slot_out[...] = jnp.broadcast_to(slot, slot_out.shape)
    place = (slot == iota((total, rows), 0)).astype(F32).astype(BF16)
    copies[1].wait()
    score = column(jax.nn.sigmoid(logit_ref[...]))
    copies[2].wait()
    weighted = (score * grad_ref[...].astype(F32)).astype(BF16)
    copies[3].wait()
    both = jnp.concatenate([tok_ref[...], weighted], axis=1)
    out[...] = dot(place, both).astype(BF16)


def unpack_kernel(slot_ref, logit_ref, back_ref, grad_out, logit_out):
    total = back_ref.shape[0]
    rows, width = grad_out.shape
    slot = jnp.transpose(slot_ref[...])[:, :1]
    place = (slot == iota((rows, total), 1)).astype(F32).astype(BF16)
    own = dot(place, back_ref[...])
    grad_out[...] = own[:, :width].astype(BF16)
    gate_dot = jnp.transpose(own[:, width:])[:1]
    logit_out[...] = (1.0 - jax.nn.sigmoid(logit_ref[...])) * gate_dot


def block_of(cut, hop, other, chips):
    chip = (cut // 2 + chips - hop) % chips
    core = cut % 2
    return 2 * chip + (1 - core if other else core)


def at(index, size):
    return pl.ds(pl.multiple_of(index * size, size), size)


def gates_kernel(chips, cut_ref, *refs):
    count = 2 * chips - 1
    near, far = refs[:count], refs[count : 2 * count]
    gate_ref, up_ref, hid_out, act_out, slope_out, send_out, keep_out, gram = refs[2 * count :]
    cut = cut_ref[0]
    width = near[0].shape[1]

    def rows_of(k):
        parts = [
            [side[0][...]] if k == 0 else [side[2 * k - 1][...], side[2 * k][...]]
            for side in (near, far)
        ]
        return jnp.concatenate([jnp.concatenate(p, axis=0) for p in parts], axis=1)

    for ref, out in ((gate_ref, act_out), (up_ref, slope_out)):
        for k in range(chips):
            mat = [ref[at(block_of(cut, k, o, chips), width), :] for o in (False, True)]
            mat = jnp.concatenate(mat, axis=0)
            if k == 0:
                out[...] = dot(rows_of(k), mat)
            else:
                out[...] += dot(rows_of(k), mat)
    gate_pre = act_out[...]
    up_pre = slope_out[...]
    sig = jax.nn.sigmoid(gate_pre)
    act = gate_pre * sig
    hidden = (act * up_pre).astype(BF16)
    act_out[...] = act
    slope_out[...] = up_pre * (sig * (1.0 + gate_pre * (1.0 - sig)))
    hid_out[...] = hidden
    gram[...] = dot(hidden, hidden, LAST)
    half = send_out.shape[0]
    keep_out[...] = gram[at(cut % 2, half), :].astype(BF16)
    send_out[...] = gram[at(1 - cut % 2, half), :].astype(BF16)


def encode(flat, width, base):
    rest = flat.shape[1] - width
    over = jnp.concatenate([flat[:, width:], jnp.zeros((8, width - rest), F32)], axis=1)
    left = jnp.concatenate([flat[:, :width], over], axis=0)
    row = iota(left.shape, 0) % 8 - base
    tail = jnp.zeros_like(left)
    for n in range(2):
        term = left.astype(BF16).astype(F32)
        tail = jnp.where(row == n, term, tail)
        left = left - term
    return tail.astype(BF16)


def decode(tail, total):
    flat = [jnp.sum(tail[8 * n : 8 * n + 8], axis=0, keepdims=True) for n in range(2)]
    return jnp.concatenate([flat[0], flat[1][:, : total - flat[0].shape[1]]], axis=1)


def down_product(down_ref, cut, near, far, hop, chips):
    width = near.shape[1]
    mat = [down_ref[:, at(block_of(cut, hop, o, chips), width)] for o in (False, True)]
    rows = jnp.concatenate([near[...], far[...]], axis=1)
    return dot(rows, jnp.concatenate(mat, axis=1), LAST)


def own_hidden_kernel(chips, cut_ref, near, far, down_ref, out):
    out[...] = down_product(down_ref, cut_ref[0], near, far, 0, chips)


def hidden_kernel(chips, cut_ref, *refs):
    near, far = refs[: chips - 1], refs[chips - 1 : 2 * chips - 2]
    down_ref, first_ref, hid_ref, act_ref, slope_ref = refs[2 * chips - 2 : 2 * chips + 3]
    both_out, tail_out, relay_out, acc = refs[2 * chips + 3 :]
    cut = cut_ref[0]
    for k in range(1, chips):
        start = first_ref if k == 1 else acc
        acc[...] = start[...] + down_product(down_ref, cut, near[k - 1], far[k - 1], k, chips)
    grad = acc[...]
    ff = grad.shape[1]
    both_out[:, :ff] = (grad * slope_ref[...]).astype(BF16)
    both_out[:, ff:] = (grad * act_ref[...]).astype(BF16)
    dots = jnp.sum(hid_ref[...].astype(F32) * grad, axis=1, keepdims=True)
    flat = jnp.transpose(jnp.broadcast_to(dots, (dots.shape[0], 128)))[:8]
    width = near[0].shape[1]
    tail_out[...] = encode(flat, width, 2 * (cut % 2))
    relay_out[...] = encode(flat, width, 4 + 2 * (cut % 2))


def part_kernel(cut_ref, both_ref, tail_ref, gate_own, gate_oth, up_own, up_oth, *refs):
    keep_out, send_out = refs[-2:]
    gate = jnp.concatenate([gate_own[...], gate_oth[...]], axis=0)
    up = jnp.concatenate([up_own[...], up_oth[...]], axis=0)
    out = dot(both_ref[...], jnp.concatenate([gate, up], axis=1), LAST).astype(BF16)
    total, width = both_ref.shape[0], keep_out.shape[1]
    keep_out[:total, :] = out[:, :width]
    send_out[:total, :] = out[:, width:]
    keep_out[total:, :] = tail_ref[...]
    send_out[total:, :] = tail_ref[...]


def part(where, both, tail, gate_mat, up_mat, width, hop, chips, after):
    rows, ff = both.shape[0], gate_mat.shape[1]
    mats = [
        pl.BlockSpec((width, ff), lambda i, w, o=o: (block_of(w[0], chips - hop, o, chips), 0))
        for o in (False, True, False, True)
    ]
    long = rows + tail.shape[0]
    out = jax.ShapeDtypeStruct((long, width), BF16)
    full = pl.BlockSpec((long, width), lambda i, w: (0, 0))
    return pl.pallas_call(
        part_kernel,
        out_shape=[out, out],
        grid_spec=pltpu.PrefetchScalarGridSpec(
            num_scalar_prefetch=1,
            grid=(1,),
            in_specs=[
                pl.BlockSpec((rows, 2 * ff), lambda i, w: (0, 0)),
                pl.BlockSpec(tail.shape, lambda i, w: (0, 0)),
            ]
            + mats
            + [pl.BlockSpec(memory_space=pl.ANY)] * len(after),
            out_specs=[full, full],
        ),
        compiler_params=pltpu.CompilerParams(vmem_limit_bytes=10 << 20),
        cost_estimate=pl.CostEstimate(
            flops=8 * rows * ff * width, bytes_accessed=6 << 20, transcendentals=0
        ),
        name="input_part",
    )(where, both, tail, gate_mat, gate_mat, up_mat, up_mat, *after)


def final_kernel(*refs):
    sums, out = refs[:-1], refs[-1]
    rows = out.shape[0]
    width = sums[0].shape[1]
    total = sums[0][...].astype(F32)
    for ref in sums[1:]:
        total = total + ref[...].astype(F32)
    out[:, :width] = total[:rows].astype(BF16)
    flat = decode(total[rows:], rows)
    lane = jnp.transpose(jnp.broadcast_to(flat, (out.shape[1] - width, rows)))
    out[:, width:] = lane.astype(BF16)


def stats_kernel(chips, cut_ref, *refs):
    near, far = refs[:chips], refs[chips : 2 * chips]
    own_k, oth_k, out, rows, gram = refs[2 * chips :]
    cut = cut_ref[0]
    width = near[0].shape[1]
    for k in range(chips):
        rows[:, at(block_of(cut, k, False, chips), width)] = near[k][...]
        rows[:, at(block_of(cut, k, True, chips), width)] = far[k][...]
    half = own_k.shape[0]
    gram[at(cut % 2, half), :] = own_k[...]
    gram[at(1 - cut % 2, half), :] = oth_k[...]
    share = out.shape[1]
    blocks = out.shape[0]
    per = BLOCK // share
    own = jnp.concatenate([rows[:, at(per * j + cut, share)] for j in range(blocks)], axis=1)
    mixed = dot(gram[...], own).astype(BF16)
    for j in range(blocks):
        out[j] = dot(
            mixed[:, j * share : (j + 1) * share], rows[:, j * BLOCK : (j + 1) * BLOCK], FIRST
        ) * (1.0 / FF)


def shards(tokens, out_grad, gate_logit, expert_ids, w_gate, w_up, w_down):
    experts = lax.axis_size("expert")
    cuts = lax.axis_size("cuts")
    chips = cuts // 2
    tok_rows, width = tokens.shape
    capacity = 2 * tok_rows // experts
    total = experts * capacity
    gate_mat, up_mat, down_mat = w_gate[0], w_up[0], w_down[0]
    ff, feats = down_mat.shape
    shape = jax.ShapeDtypeStruct
    cut = lax.axis_index("cuts").astype(jnp.int32)
    where = cut.reshape(1)

    def hop(x, k):
        if k == 0:
            return x
        return lax.ppermute(
            x, "cuts", [(2 * i + c, 2 * ((i + k) % chips) + c) for i in range(chips) for c in (0, 1)]
        )

    def swap(x):
        return lax.ppermute(x, "cuts", [(i, i ^ 1) for i in range(cuts)])

    def exchange(x):
        return lax.all_to_all(x, "expert", split_axis=0, concat_axis=0, tiled=True)

    ids = expert_ids.reshape(1, tok_rows)
    logit = gate_logit.reshape(1, tok_rows)
    packed, slot = pl.pallas_call(
        functools.partial(pack_kernel, capacity),
        out_shape=[shape((total, 2 * width), BF16), shape((8, tok_rows), jnp.int32)],
        in_specs=[pl.BlockSpec(memory_space=pltpu.SMEM)]
        + [pl.BlockSpec(memory_space=pltpu.HBM)] * 4,
        out_specs=[whole()] * 2,
        scratch_shapes=[
            VMEM((1, tok_rows), jnp.int32),
            VMEM((1, tok_rows), F32),
            VMEM((tok_rows, width), BF16),
            VMEM((tok_rows, width), BF16),
            pltpu.SemaphoreType.DMA((4,)),
        ],
        compiler_params=pltpu.CompilerParams(vmem_limit_bytes=8 << 20),
        name="pack",
    )(where, ids, logit, tokens, out_grad)
    routed = exchange(packed.reshape(experts, capacity, 2 * width)).reshape(total, 2 * width)
    tok_in, wt_in = routed[:, :width], routed[:, width:]
    mid = total // 2
    ahead_top, back_low = hop(tok_in[:mid], 1), hop(tok_in[mid:], chips - 1)
    ahead_low, back_top = hop(tok_in[mid:], 1), hop(tok_in[:mid], chips - 1)
    tok_near = [tok_in, ahead_top, ahead_low]
    tok_near += [hop(ahead_top, 1), hop(back_low, chips - 1), back_top, back_low]
    tok_far = [swap(x) for x in tok_near]
    wt_near = [hop(wt_in, k) for k in range(chips)]
    wt_swap = swap(wt_in)

    half = total // 2
    hidden, act, slope, gram_send, gram_keep = call(
        functools.partial(gates_kernel, chips),
        [
            shape((total, ff), BF16),
            shape((total, ff), F32),
            shape((total, ff), F32),
            shape((half, total), BF16),
            shape((half, total), BF16),
        ],
        (where, *tok_near, *tok_far, gate_mat, up_mat),
        0,
        "gates",
        scratch=[VMEM((total, total), F32)],
        limit=18,
        light=True,
    )
    def add(x, y):
        return (x.astype(F32) + y.astype(F32)).astype(BF16)

    def chip_swap(x, bit):
        return lax.ppermute(
            x, "cuts", [(2 * i + c, 2 * (i ^ bit) + c) for i in range(chips) for c in (0, 1)]
        )

    gram_sum = add(gram_keep, swap(gram_send))
    (first,) = call(
        functools.partial(own_hidden_kernel, chips),
        [shape((total, ff), F32)],
        (where, wt_in, wt_swap, down_mat),
        4 * total * width * ff,
        "own_hidden_grad",
        after=(hidden,),
        light=True,
    )
    wt_late, first = lax.optimization_barrier((wt_near[1:], first))
    wt_far = [wt_swap] + [swap(x) for x in wt_late]
    both, tail, relay_tail = call(
        functools.partial(hidden_kernel, chips),
        [
            shape((total, 2 * ff), BF16),
            shape((16, width), BF16),
            shape((16, width), BF16),
        ],
        (where, *wt_near[1:], *wt_far[1:], down_mat, first, hidden, act, slope),
        2 * total * (feats - 2 * width) * ff,
        "hidden_grad",
        scratch=[VMEM((total, ff), F32)],
    )

    def pieces(k, tail, after):
        keep, send = part(where, both, tail, gate_mat, up_mat, width, k, chips, after)
        return keep, swap(send)

    def total_of(*terms):
        return sum(x.astype(F32) for x in terms).astype(BF16)

    through = total_of(*pieces(2, relay_tail, ()))
    right = pieces(1, tail, ())
    left = pieces(chips - 1, tail, (through,))
    own = total_of(*pieces(0, tail, (through,)))
    top, low = hop(through[:mid], 1), hop(through[mid:], chips - 1)
    right = total_of(*right, jnp.pad(top, ((0, own.shape[0] - mid), (0, 0))))
    left = total_of(*left, jnp.pad(low, ((mid, 0), (0, 0))))
    sums = [own, hop(right, 1), hop(left, chips - 1)]
    gram_sum, _ = lax.optimization_barrier((gram_sum, left))
    gram_sum = add(gram_sum, chip_swap(gram_sum, 1))
    (payload,) = call(
        final_kernel,
        [shape((total, width + 128), BF16)],
        tuple(sums),
        0,
        "final",
        scalars=0,
        limit=8,
        after=(gram_sum,),
    )
    gram_sum, payload = lax.optimization_barrier((gram_sum, payload))
    gram_sum = add(gram_sum, chip_swap(gram_sum, 2))
    gram_other = swap(gram_sum)
    blocks = feats // BLOCK
    (stats,) = call(
        functools.partial(stats_kernel, chips),
        [shape((blocks, BLOCK // cuts, BLOCK), F32)],
        (where, *wt_near, *wt_far, gram_sum, gram_other),
        4 * total * total * feats // cuts + 2 * total * BLOCK * feats // cuts,
        "stats",
        scratch=[VMEM((total, feats), BF16), VMEM((total, total), BF16)],
        after=(payload,),
    )
    back = exchange(payload.reshape(experts, capacity, width + 128)).reshape(total, width + 128)
    input_grad, logit_grad = call(
        unpack_kernel,
        [shape((tok_rows, width), BF16), shape((1, tok_rows), F32)],
        (slot, logit, back),
        2 * tok_rows * total * (width + 128),
        "unpack",
        scalars=0,
    )
    return input_grad, logit_grad.reshape(tok_rows), stats[None]


def solution(mesh):
    return jax.shard_map(
        shards,
        mesh=mesh,
        in_specs=(
            P("expert", "cuts"),
            P("expert", "cuts"),
            P("expert"),
            P("expert", None),
            P("expert", None, "cuts"),
            P("expert", None, "cuts"),
            P("expert", "cuts", None),
        ),
        out_specs=(P("expert", "cuts"), P("expert"), P("expert", None, "cuts", None)),
        check_vma=False,
    )
```

```python
import functools

import jax
import jax.numpy as jnp
from jax import lax
from jax.experimental import pallas as pl
from jax.experimental.pallas import tpu as pltpu
from jax.sharding import PartitionSpec as P

FF = 4096
BLOCK = 1024
F32 = jnp.float32
BF16 = jnp.bfloat16
VMEM = pltpu.VMEM
LAST = (((1,), (1,)), ((), ()))
FIRST = (((0,), (0,)), ((), ()))


def dot(a, b, dims=(((1,), (0,)), ((), ()))):
    return lax.dot_general(a, b, dims, preferred_element_type=F32)


def iota(shape, dim):
    return lax.broadcasted_iota(jnp.int32, shape, dim)


def whole():
    return pl.BlockSpec(memory_space=VMEM)


def call(body, out, inputs, flops=0, name=None, scratch=(), scalars=1, limit=14, after=(), light=True):
    moved = sum(x.size * x.dtype.itemsize for x in inputs) + sum(
        o.size * o.dtype.itemsize for o in out
    )
    if light:
        flops, moved = 0, 0
    specs = [pl.BlockSpec(memory_space=pltpu.SMEM)] * scalars
    specs += [whole()] * (len(inputs) - scalars)
    specs += [pl.BlockSpec(memory_space=pl.ANY)] * len(after)
    count = len(inputs)

    def kernel(*refs):
        body(*refs[:count], *refs[count + len(after) :])

    return pl.pallas_call(
        kernel,
        out_shape=out,
        in_specs=specs,
        out_specs=[whole()] * len(out),
        scratch_shapes=list(scratch),
        compiler_params=pltpu.CompilerParams(vmem_limit_bytes=limit << 20),
        cost_estimate=pl.CostEstimate(flops=flops, bytes_accessed=moved, transcendentals=0),
        name=name,
    )(*inputs, *after)


def pack_kernel(capacity, cut_ref, ids_ref, tok_ref, wt_ref, out, slot_out):
    ids = ids_ref[...]
    rows, width = tok_ref.shape
    total = out.shape[0]
    mine = ids == iota((total // capacity, rows), 0)
    earlier = (iota((rows, rows), 0) < iota((rows, rows), 1)).astype(F32).astype(BF16)
    before = dot(mine.astype(F32).astype(BF16), earlier)
    arrival = jnp.sum(jnp.where(mine, before, 0.0), axis=0, keepdims=True)
    slot = ids * capacity + arrival.astype(jnp.int32)
    slot_out[...] = jnp.broadcast_to(slot, slot_out.shape)
    place = (slot == iota((total, rows), 0)).astype(F32).astype(BF16)
    both = jnp.concatenate([tok_ref[...], wt_ref[...]], axis=1)
    out[...] = dot(place, both).astype(BF16)


def unpack_kernel(slot_ref, logit_ref, back_ref, grad_out, logit_out):
    total = back_ref.shape[0]
    rows, width = grad_out.shape
    slot = jnp.transpose(slot_ref[...])[:, :1]
    place = (slot == iota((rows, total), 1)).astype(F32).astype(BF16)
    own = dot(place, back_ref[...])
    grad_out[...] = own[:, :width].astype(BF16)
    gate_dot = jnp.transpose(own[:, width:])[:1]
    logit_out[...] = (1.0 - jax.nn.sigmoid(logit_ref[...])) * gate_dot


def block_of(cut, hop, other, chips):
    chip = (cut // 2 + chips - hop) % chips
    core = cut % 2
    return 2 * chip + (1 - core if other else core)


def at(index, size):
    return pl.ds(pl.multiple_of(index * size, size), size)


def gates_kernel(chips, cut_ref, *refs):
    near, far_own, far_ref = refs[:chips], refs[chips], refs[chips + 1]
    gate_ref, up_ref, hid_out, act_out, slope_out, send_out, keep_out, gram = refs[chips + 2 :]
    cut = cut_ref[0]
    width = near[0].shape[1]
    for ref, out in ((gate_ref, act_out), (up_ref, slope_out)):
        for k in range(chips):
            far = far_ref[k - 1] if k else far_own[...]
            rows = jnp.concatenate([near[k][...], far], axis=1)
            mat = [ref[at(block_of(cut, k, o, chips), width), :] for o in (False, True)]
            mat = jnp.concatenate(mat, axis=0)
            if k == 0:
                out[...] = dot(rows, mat)
            else:
                out[...] += dot(rows, mat)
    gate_pre = act_out[...]
    up_pre = slope_out[...]
    sig = jax.nn.sigmoid(gate_pre)
    act = gate_pre * sig
    hidden = (act * up_pre).astype(BF16)
    act_out[...] = act
    slope_out[...] = up_pre * (sig * (1.0 + gate_pre * (1.0 - sig)))
    hid_out[...] = hidden
    gram[...] = dot(hidden, hidden, LAST)
    half = send_out.shape[0]
    keep_out[...] = gram[at(cut % 2, half), :].astype(BF16)
    send_out[...] = gram[at(1 - cut % 2, half), :].astype(BF16)


def encode(flat, width, base):
    rest = flat.shape[1] - width
    over = jnp.concatenate([flat[:, width:], jnp.zeros((8, width - rest), F32)], axis=1)
    left = jnp.concatenate([flat[:, :width], over], axis=0)
    row = iota(left.shape, 0) % 8 - base
    tail = jnp.zeros_like(left)
    for n in range(2):
        term = left.astype(BF16).astype(F32)
        tail = jnp.where(row == n, term, tail)
        left = left - term
    return tail.astype(BF16)


def decode(tail, total):
    flat = [jnp.sum(tail[8 * n : 8 * n + 8], axis=0, keepdims=True) for n in range(2)]
    return jnp.concatenate([flat[0], flat[1][:, : total - flat[0].shape[1]]], axis=1)


def down_product(down_ref, cut, near, far, hop, chips):
    width = near.shape[1]
    mat = [down_ref[:, at(block_of(cut, hop, o, chips), width)] for o in (False, True)]
    rows = jnp.concatenate([near[...], far[...]], axis=1)
    return dot(rows, jnp.concatenate(mat, axis=1), LAST)


def own_hidden_kernel(chips, cut_ref, near, far, down_ref, out):
    out[...] = down_product(down_ref, cut_ref[0], near, far, 0, chips)


def hidden_kernel(chips, cut_ref, *refs):
    near, far = refs[: chips - 1], refs[chips - 1 : 2 * chips - 2]
    down_ref, first_ref, hid_ref, act_ref, slope_ref = refs[2 * chips - 2 : 2 * chips + 3]
    both_out, tail_out, acc = refs[2 * chips + 3 :]
    cut = cut_ref[0]
    for k in range(1, chips):
        start = first_ref if k == 1 else acc
        acc[...] = start[...] + down_product(down_ref, cut, near[k - 1], far[k - 1], k, chips)
    grad = acc[...]
    ff = grad.shape[1]
    both_out[:, :ff] = (grad * slope_ref[...]).astype(BF16)
    both_out[:, ff:] = (grad * act_ref[...]).astype(BF16)
    dots = jnp.sum(hid_ref[...].astype(F32) * grad, axis=1, keepdims=True)
    flat = jnp.transpose(jnp.broadcast_to(dots, (dots.shape[0], 128)))[:8]
    width = near[0].shape[1]
    tail_out[0] = encode(flat, width, 2 * (cut % 2))
    tail_out[1] = encode(flat, width, 4 + 2 * (cut % 2))


def part_kernel(cut_ref, both_ref, tail_ref, gate_own, gate_oth, up_own, up_oth, *refs):
    keep_out, send_out = refs[-2:]
    gate = jnp.concatenate([gate_own[...], gate_oth[...]], axis=0)
    up = jnp.concatenate([up_own[...], up_oth[...]], axis=0)
    out = dot(both_ref[...], jnp.concatenate([gate, up], axis=1), LAST).astype(BF16)
    total, width = both_ref.shape[0], keep_out.shape[2]
    keep_out[0, :total, :] = out[:, :width]
    send_out[0, :total, :] = out[:, width:]
    keep_out[0, total:, :] = tail_ref[0]
    send_out[0, total:, :] = tail_ref[0]


def part(where, both, tail, gate_mat, up_mat, width, count, hop_of, chips, after=()):
    rows, ff = both.shape[0], gate_mat.shape[1]
    mats = [
        pl.BlockSpec(
            (width, ff), lambda i, w, o=o: (block_of(w[0], chips - hop_of(i), o, chips), 0)
        )
        for o in (False, True, False, True)
    ]
    long = rows + tail.shape[1]
    out = jax.ShapeDtypeStruct((count, long, width), BF16)
    block = pl.BlockSpec((1, long, width), lambda i, w: (i, 0, 0))
    return pl.pallas_call(
        part_kernel,
        out_shape=[out, out],
        grid_spec=pltpu.PrefetchScalarGridSpec(
            num_scalar_prefetch=1,
            grid=(count,),
            in_specs=[
                pl.BlockSpec((rows, 2 * ff), lambda i, w: (0, 0)),
                pl.BlockSpec(
                    (1,) + tail.shape[1:],
                    lambda i, w: (jnp.where(hop_of(i) == chips // 2, 1, 0), 0, 0),
                ),
            ]
            + mats
            + [pl.BlockSpec(memory_space=pl.ANY)] * len(after),
            out_specs=[block, block],
        ),
        compiler_params=pltpu.CompilerParams(vmem_limit_bytes=12 << 20),
        cost_estimate=pl.CostEstimate(
            flops=8 * rows * ff * width * count,
            bytes_accessed=(4 << 20) * count,
            transcendentals=0,
        ),
        name="input_part",
    )(where, both, tail, gate_mat, gate_mat, up_mat, up_mat, *after)


def final_kernel(*refs):
    sums, out = refs[:-1], refs[-1]
    rows = out.shape[0]
    width = sums[0].shape[1]
    total = sums[0][...].astype(F32)
    for ref in sums[1:]:
        total = total + ref[...].astype(F32)
    out[:, :width] = total[:rows].astype(BF16)
    flat = decode(total[rows:], rows)
    lane = jnp.transpose(jnp.broadcast_to(flat, (out.shape[1] - width, rows)))
    out[:, width:] = lane.astype(BF16)


def stats_kernel(chips, cut_ref, *refs):
    near, far = refs[:chips], refs[chips : 2 * chips]
    own_k, oth_k, out, rows, gram = refs[2 * chips :]
    cut = cut_ref[0]
    width = near[0].shape[1]
    for k in range(chips):
        rows[:, at(block_of(cut, k, False, chips), width)] = near[k][...]
        rows[:, at(block_of(cut, k, True, chips), width)] = far[k][...]
    half = own_k.shape[0]
    gram[at(cut % 2, half), :] = own_k[...]
    gram[at(1 - cut % 2, half), :] = oth_k[...]
    share = out.shape[1]
    blocks = out.shape[0]
    per = BLOCK // share
    own = jnp.concatenate([rows[:, at(per * j + cut, share)] for j in range(blocks)], axis=1)
    mixed = dot(gram[...], own).astype(BF16)
    for j in range(blocks):
        out[j] = dot(
            mixed[:, j * share : (j + 1) * share], rows[:, j * BLOCK : (j + 1) * BLOCK], FIRST
        ) * (1.0 / FF)


def shards(tokens, out_grad, gate_logit, expert_ids, w_gate, w_up, w_down):
    experts = lax.axis_size("expert")
    cuts = lax.axis_size("cuts")
    chips = cuts // 2
    tok_rows, width = tokens.shape
    capacity = 2 * tok_rows // experts
    total = experts * capacity
    gate_mat, up_mat, down_mat = w_gate[0], w_up[0], w_down[0]
    ff, feats = down_mat.shape
    shape = jax.ShapeDtypeStruct
    cut = lax.axis_index("cuts").astype(jnp.int32)
    where = cut.reshape(1)

    def hop(x, k):
        if k == 0:
            return x
        return lax.ppermute(
            x, "cuts", [(2 * i + c, 2 * ((i + k) % chips) + c) for i in range(chips) for c in (0, 1)]
        )

    def swap(x):
        return lax.ppermute(x, "cuts", [(i, i ^ 1) for i in range(cuts)])

    def exchange(x):
        return lax.all_to_all(x, "expert", split_axis=0, concat_axis=0, tiled=True)

    ids = expert_ids.reshape(1, tok_rows)
    logit = gate_logit.reshape(1, tok_rows)
    score = jax.nn.sigmoid(gate_logit)
    weighted = (score[:, None] * out_grad.astype(F32)).astype(BF16)
    packed, slot = call(
        functools.partial(pack_kernel, capacity),
        [shape((total, 2 * width), BF16), shape((8, tok_rows), jnp.int32)],
        (where, ids, tokens, weighted),
        0,
        "pack",
        limit=8,
    )
    routed = exchange(packed.reshape(experts, capacity, 2 * width)).reshape(total, 2 * width)
    tok_in, wt_in = routed[:, :width], routed[:, width:]
    mid = total // 2
    tok_near = [hop(tok_in, k) for k in range(chips)]
    tok_far = [swap(tok_in), swap(jnp.stack(tok_near[1:]))]
    wt_near = [hop(wt_in, k) for k in range(chips)]
    wt_swap = swap(wt_in)
    half = total // 2
    hidden, act, slope, gram_send, gram_keep = call(
        functools.partial(gates_kernel, chips),
        [
            shape((total, ff), BF16),
            shape((total, ff), F32),
            shape((total, ff), F32),
            shape((half, total), BF16),
            shape((half, total), BF16),
        ],
        (where, *tok_near, *tok_far, gate_mat, up_mat),
        0,
        "gates",
        scratch=[VMEM((total, total), F32)],
        limit=18,
        light=True,
    )
    def add(x, y):
        return (x.astype(F32) + y.astype(F32)).astype(BF16)

    def chip_swap(x, bit):
        return lax.ppermute(
            x, "cuts", [(2 * i + c, 2 * (i ^ bit) + c) for i in range(chips) for c in (0, 1)]
        )

    gram_sum = add(gram_keep, swap(gram_send))
    (first,) = call(
        functools.partial(own_hidden_kernel, chips),
        [shape((total, ff), F32)],
        (where, wt_in, wt_swap, down_mat),
        4 * total * width * ff,
        "own_hidden_grad",
        after=(hidden,),
        light=True,
    )
    wt_far = [wt_swap]
    for k in range(1, chips):
        late, _ = lax.optimization_barrier((wt_near[k], first))
        wt_far.append(swap(late))
    both, tails = call(
        functools.partial(hidden_kernel, chips),
        [
            shape((total, 2 * ff), BF16),
            shape((2, 16, width), BF16),
        ],
        (where, *wt_near[1:], *wt_far[1:], down_mat, first, hidden, act, slope),
        2 * total * (feats - 2 * width) * ff,
        "hidden_grad",
        scratch=[VMEM((total, ff), F32)],
    )

    def total_of(*terms):
        return sum(x.astype(F32) for x in terms).astype(BF16)

    keep, send = part(
        where, both, tails, gate_mat, up_mat, width, chips - 1, lambda i: i + 1, chips
    )
    gram_sum, _ = lax.optimization_barrier((gram_sum, wt_near[-1]))
    gram_sum = add(gram_sum, chip_swap(gram_sum, 1))
    send, gram_sum = lax.optimization_barrier((send, gram_sum))
    recv = swap(send)
    through = total_of(keep[1], recv[1])
    long = send.shape[1]
    top, low = hop(through[:mid], 1), hop(through[mid:], chips - 1)
    right = total_of(keep[0], recv[0], jnp.pad(top, ((0, long - mid), (0, 0))))
    left = total_of(keep[2], recv[2], jnp.pad(low, ((mid, 0), (0, 0))))
    keep, send = part(
        where, both, tails, gate_mat, up_mat, width, 1, lambda i: 0, chips, (through,)
    )
    own = total_of(keep[0], swap(send)[0])
    sums = [own, hop(right, 1), hop(left, chips - 1)]
    (payload,) = call(
        final_kernel,
        [shape((total, width + 128), BF16)],
        tuple(sums),
        0,
        "final",
        scalars=0,
        limit=8,
        after=(gram_sum,),
    )
    gram_sum, payload = lax.optimization_barrier((gram_sum, payload))
    gram_sum = add(gram_sum, chip_swap(gram_sum, 2))
    gram_other = swap(gram_sum)
    blocks = feats // BLOCK
    (stats,) = call(
        functools.partial(stats_kernel, chips),
        [shape((blocks, BLOCK // cuts, BLOCK), F32)],
        (where, *wt_near, *wt_far, gram_sum, gram_other),
        4 * total * total * feats // cuts + 2 * total * BLOCK * feats // cuts,
        "stats",
        scratch=[VMEM((total, feats), BF16), VMEM((total, total), BF16)],
        after=(payload,),
    )
    back = exchange(payload.reshape(experts, capacity, width + 128)).reshape(total, width + 128)
    input_grad, logit_grad = call(
        unpack_kernel,
        [shape((tok_rows, width), BF16), shape((1, tok_rows), F32)],
        (slot, logit, back),
        2 * tok_rows * total * (width + 128),
        "unpack",
        scalars=0,
    )
    return input_grad, logit_grad.reshape(tok_rows), stats[None]


def solution(mesh):
    return jax.shard_map(
        shards,
        mesh=mesh,
        in_specs=(
            P("expert", "cuts"),
            P("expert", "cuts"),
            P("expert"),
            P("expert", None),
            P("expert", None, "cuts"),
            P("expert", None, "cuts"),
            P("expert", "cuts", None),
        ),
        out_specs=(P("expert", "cuts"), P("expert"), P("expert", None, "cuts", None)),
        check_vma=False,
    )
```

```python
import functools

import jax
import jax.numpy as jnp
from jax import lax
from jax.experimental import pallas as pl
from jax.experimental.pallas import tpu as pltpu
from jax.sharding import PartitionSpec as P

FF = 4096
BLOCK = 1024
F32 = jnp.float32
BF16 = jnp.bfloat16
VMEM = pltpu.VMEM
LAST = (((1,), (1,)), ((), ()))
FIRST = (((0,), (0,)), ((), ()))


def dot(a, b, dims=(((1,), (0,)), ((), ()))):
    return lax.dot_general(a, b, dims, preferred_element_type=F32)


def iota(shape, dim):
    return lax.broadcasted_iota(jnp.int32, shape, dim)


def whole():
    return pl.BlockSpec(memory_space=VMEM)


def call(body, out, inputs, flops=0, name=None, scratch=(), scalars=1, limit=14, after=(), light=True):
    moved = sum(x.size * x.dtype.itemsize for x in inputs) + sum(
        o.size * o.dtype.itemsize for o in out
    )
    if light:
        flops, moved = 0, 0
    specs = [pl.BlockSpec(memory_space=pltpu.SMEM)] * scalars
    specs += [whole()] * (len(inputs) - scalars)
    specs += [pl.BlockSpec(memory_space=pl.ANY)] * len(after)
    count = len(inputs)

    def kernel(*refs):
        body(*refs[:count], *refs[count + len(after) :])

    return pl.pallas_call(
        kernel,
        out_shape=out,
        in_specs=specs,
        out_specs=[whole()] * len(out),
        scratch_shapes=list(scratch),
        compiler_params=pltpu.CompilerParams(vmem_limit_bytes=limit << 20),
        cost_estimate=pl.CostEstimate(flops=flops, bytes_accessed=moved, transcendentals=0),
        name=name,
    )(*inputs, *after)


def pack_kernel(capacity, cut_ref, ids_ref, tok_ref, wt_ref, tok_out, wt_out, slot_out):
    ids = ids_ref[...]
    rows = ids.shape[1]
    total = tok_out.shape[0]
    mine = ids == iota((total // capacity, rows), 0)
    earlier = (iota((rows, rows), 0) < iota((rows, rows), 1)).astype(F32).astype(BF16)
    before = dot(mine.astype(F32).astype(BF16), earlier)
    arrival = jnp.sum(jnp.where(mine, before, 0.0), axis=0, keepdims=True)
    slot = ids * capacity + arrival.astype(jnp.int32)
    slot_out[...] = jnp.broadcast_to(slot, slot_out.shape)
    place = (slot == iota((total, rows), 0)).astype(F32).astype(BF16)
    tok_out[...] = dot(place, tok_ref[...]).astype(BF16)
    wt_out[...] = dot(place, wt_ref[...]).astype(BF16)


def unpack_kernel(slot_ref, logit_ref, back_ref, grad_out, logit_out):
    total = back_ref.shape[0]
    rows, width = grad_out.shape
    slot = jnp.transpose(slot_ref[...])[:, :1]
    place = (slot == iota((rows, total), 1)).astype(F32).astype(BF16)
    own = dot(place, back_ref[...])
    grad_out[...] = own[:, :width].astype(BF16)
    gate_dot = jnp.transpose(own[:, width:])[:1]
    logit_out[...] = (1.0 - jax.nn.sigmoid(logit_ref[...])) * gate_dot


def block_of(cut, hop, other, chips):
    chip = (cut // 2 + chips - hop) % chips
    core = cut % 2
    return 2 * chip + (1 - core if other else core)


def at(index, size):
    return pl.ds(pl.multiple_of(index * size, size), size)


def gates_kernel(chips, cut_ref, *refs):
    near, far = refs[:chips], refs[chips : 2 * chips]
    gate_ref, up_ref, hid_out, act_out, slope_out, send_out, keep_out, gram = refs[2 * chips :]
    cut = cut_ref[0]
    width = near[0].shape[1]
    for ref, out in ((gate_ref, act_out), (up_ref, slope_out)):
        for k in range(chips):
            rows = jnp.concatenate([near[k][...], far[k][...]], axis=1)
            mat = [ref[at(block_of(cut, k, o, chips), width), :] for o in (False, True)]
            mat = jnp.concatenate(mat, axis=0)
            if k == 0:
                out[...] = dot(rows, mat)
            else:
                out[...] += dot(rows, mat)
    gate_pre = act_out[...]
    up_pre = slope_out[...]
    sig = jax.nn.sigmoid(gate_pre)
    act = gate_pre * sig
    hidden = (act * up_pre).astype(BF16)
    act_out[...] = act
    slope_out[...] = up_pre * (sig * (1.0 + gate_pre * (1.0 - sig)))
    hid_out[...] = hidden
    gram[...] = dot(hidden, hidden, LAST)
    half = send_out.shape[0]
    keep_out[...] = gram[at(cut % 2, half), :].astype(BF16)
    send_out[...] = gram[at(1 - cut % 2, half), :].astype(BF16)


def encode(flat, width, base):
    rest = flat.shape[1] - width
    over = jnp.concatenate([flat[:, width:], jnp.zeros((8, width - rest), F32)], axis=1)
    left = jnp.concatenate([flat[:, :width], over], axis=0)
    row = iota(left.shape, 0) % 8 - base
    tail = jnp.zeros_like(left)
    for n in range(2):
        term = left.astype(BF16).astype(F32)
        tail = jnp.where(row == n, term, tail)
        left = left - term
    return tail.astype(BF16)


def decode(tail, total):
    flat = [jnp.sum(tail[8 * n : 8 * n + 8], axis=0, keepdims=True) for n in range(2)]
    return jnp.concatenate([flat[0], flat[1][:, : total - flat[0].shape[1]]], axis=1)


def down_product(down_ref, cut, near, far, hop, chips):
    width = near.shape[1]
    mat = [down_ref[:, at(block_of(cut, hop, o, chips), width)] for o in (False, True)]
    rows = jnp.concatenate([near[...], far[...]], axis=1)
    return dot(rows, jnp.concatenate(mat, axis=1), LAST)


def own_hidden_kernel(chips, cut_ref, near, far, down_ref, out):
    out[...] = down_product(down_ref, cut_ref[0], near, far, 0, chips)


def hidden_kernel(chips, cut_ref, *refs):
    near, far = refs[: chips - 1], refs[chips - 1 : 2 * chips - 2]
    down_ref, first_ref, hid_ref, act_ref, slope_ref = refs[2 * chips - 2 : 2 * chips + 3]
    both_out, tail_out, acc = refs[2 * chips + 3 :]
    cut = cut_ref[0]
    for k in range(1, chips):
        start = first_ref if k == 1 else acc
        acc[...] = start[...] + down_product(down_ref, cut, near[k - 1], far[k - 1], k, chips)
    grad = acc[...]
    ff = grad.shape[1]
    both_out[:, :ff] = (grad * slope_ref[...]).astype(BF16)
    both_out[:, ff:] = (grad * act_ref[...]).astype(BF16)
    dots = jnp.sum(hid_ref[...].astype(F32) * grad, axis=1, keepdims=True)
    flat = jnp.transpose(jnp.broadcast_to(dots, (dots.shape[0], 128)))[:8]
    width = near[0].shape[1]
    tail_out[0] = encode(flat, width, 2 * (cut % 2))
    tail_out[1] = encode(flat, width, 4 + 2 * (cut % 2))


def part_kernel(cut_ref, both_ref, tail_ref, gate_own, gate_oth, up_own, up_oth, *refs):
    keep_out, send_out = refs[-2:]
    gate = jnp.concatenate([gate_own[...], gate_oth[...]], axis=0)
    up = jnp.concatenate([up_own[...], up_oth[...]], axis=0)
    out = dot(both_ref[...], jnp.concatenate([gate, up], axis=1), LAST).astype(BF16)
    total, width = both_ref.shape[0], keep_out.shape[2]
    keep_out[0, :total, :] = out[:, :width]
    send_out[0, :total, :] = out[:, width:]
    keep_out[0, total:, :] = tail_ref[0]
    send_out[0, total:, :] = tail_ref[0]


def part(where, both, tail, gate_mat, up_mat, width, count, hop_of, chips, after=()):
    rows, ff = both.shape[0], gate_mat.shape[1]
    mats = [
        pl.BlockSpec(
            (width, ff), lambda i, w, o=o: (block_of(w[0], chips - hop_of(i), o, chips), 0)
        )
        for o in (False, True, False, True)
    ]
    long = rows + tail.shape[1]
    out = jax.ShapeDtypeStruct((count, long, width), BF16)
    block = pl.BlockSpec((1, long, width), lambda i, w: (i, 0, 0))
    return pl.pallas_call(
        part_kernel,
        out_shape=[out, out],
        grid_spec=pltpu.PrefetchScalarGridSpec(
            num_scalar_prefetch=1,
            grid=(count,),
            in_specs=[
                pl.BlockSpec((rows, 2 * ff), lambda i, w: (0, 0)),
                pl.BlockSpec(
                    (1,) + tail.shape[1:],
                    lambda i, w: (jnp.where(hop_of(i) == chips // 2, 1, 0), 0, 0),
                ),
            ]
            + mats
            + [pl.BlockSpec(memory_space=pl.ANY)] * len(after),
            out_specs=[block, block],
        ),
        compiler_params=pltpu.CompilerParams(vmem_limit_bytes=12 << 20),
        cost_estimate=pl.CostEstimate(
            flops=8 * rows * ff * width * count,
            bytes_accessed=(4 << 20) * count,
            transcendentals=0,
        ),
        name="input_part",
    )(where, both, tail, gate_mat, gate_mat, up_mat, up_mat, *after)


def final_kernel(*refs):
    sums, out = refs[:-1], refs[-1]
    rows = out.shape[0]
    width = sums[0].shape[1]
    total = sums[0][...].astype(F32)
    for ref in sums[1:]:
        total = total + ref[...].astype(F32)
    out[:, :width] = total[:rows].astype(BF16)
    flat = decode(total[rows:], rows)
    lane = jnp.transpose(jnp.broadcast_to(flat, (out.shape[1] - width, rows)))
    out[:, width:] = lane.astype(BF16)


def stats_kernel(chips, cut_ref, *refs):
    near, far = refs[:chips], refs[chips : 2 * chips]
    own_k, oth_k, out, rows, gram = refs[2 * chips :]
    cut = cut_ref[0]
    width = near[0].shape[1]
    for k in range(chips):
        rows[:, at(block_of(cut, k, False, chips), width)] = near[k][...]
        rows[:, at(block_of(cut, k, True, chips), width)] = far[k][...]
    half = own_k.shape[0]
    gram[at(cut % 2, half), :] = own_k[...]
    gram[at(1 - cut % 2, half), :] = oth_k[...]
    share = out.shape[1]
    blocks = out.shape[0]
    per = BLOCK // share
    own = jnp.concatenate([rows[:, at(per * j + cut, share)] for j in range(blocks)], axis=1)
    mixed = dot(gram[...], own).astype(BF16)
    for j in range(blocks):
        out[j] = dot(
            mixed[:, j * share : (j + 1) * share], rows[:, j * BLOCK : (j + 1) * BLOCK], FIRST
        ) * (1.0 / FF)


def shards(tokens, out_grad, gate_logit, expert_ids, w_gate, w_up, w_down):
    experts = lax.axis_size("expert")
    cuts = lax.axis_size("cuts")
    chips = cuts // 2
    tok_rows, width = tokens.shape
    capacity = 2 * tok_rows // experts
    total = experts * capacity
    gate_mat, up_mat, down_mat = w_gate[0], w_up[0], w_down[0]
    ff, feats = down_mat.shape
    shape = jax.ShapeDtypeStruct
    cut = lax.axis_index("cuts").astype(jnp.int32)
    where = cut.reshape(1)

    def hop(x, k):
        if k == 0:
            return x
        return lax.ppermute(
            x, "cuts", [(2 * i + c, 2 * ((i + k) % chips) + c) for i in range(chips) for c in (0, 1)]
        )

    def swap(x):
        return lax.ppermute(x, "cuts", [(i, i ^ 1) for i in range(cuts)])

    def exchange(x):
        return lax.all_to_all(x, "expert", split_axis=0, concat_axis=0, tiled=True)

    ids = expert_ids.reshape(1, tok_rows)
    logit = gate_logit.reshape(1, tok_rows)
    score = jax.nn.sigmoid(gate_logit)
    weighted = (score[:, None] * out_grad.astype(F32)).astype(BF16)
    tok_pack, wt_pack, slot = call(
        functools.partial(pack_kernel, capacity),
        [
            shape((total, width), BF16),
            shape((total, width), BF16),
            shape((8, tok_rows), jnp.int32),
        ],
        (where, ids, tokens, weighted),
        0,
        "pack",
        limit=8,
    )
    tok_in = exchange(tok_pack.reshape(experts, capacity, width)).reshape(total, width)
    wt_pack, tok_in = lax.optimization_barrier((wt_pack, tok_in))
    wt_in = exchange(wt_pack.reshape(experts, capacity, width)).reshape(total, width)
    mid = total // 2
    tok_near = [hop(tok_in, k) for k in range(chips)]
    tok_far = [swap(x) for x in tok_near]
    wt_in, _ = lax.optimization_barrier((wt_in, tok_far))
    wt_near = [hop(wt_in, k) for k in range(chips)]
    wt_swap = swap(wt_in)
    half = total // 2
    hidden, act, slope, gram_send, gram_keep = call(
        functools.partial(gates_kernel, chips),
        [
            shape((total, ff), BF16),
            shape((total, ff), F32),
            shape((total, ff), F32),
            shape((half, total), BF16),
            shape((half, total), BF16),
        ],
        (where, *tok_near, *tok_far, gate_mat, up_mat),
        0,
        "gates",
        scratch=[VMEM((total, total), F32)],
        limit=18,
        after=(wt_swap,),
        light=True,
    )
    def add(x, y):
        return (x.astype(F32) + y.astype(F32)).astype(BF16)

    def chip_swap(x, bit):
        return lax.ppermute(
            x, "cuts", [(2 * i + c, 2 * (i ^ bit) + c) for i in range(chips) for c in (0, 1)]
        )

    gram_sum = add(gram_keep, swap(gram_send))
    (first,) = call(
        functools.partial(own_hidden_kernel, chips),
        [shape((total, ff), F32)],
        (where, wt_in, wt_swap, down_mat),
        4 * total * width * ff,
        "own_hidden_grad",
        after=(hidden,),
        light=True,
    )
    wt_far = [wt_swap]
    for k in range(1, chips):
        late, _ = lax.optimization_barrier((wt_near[k], first))
        wt_far.append(swap(late))
    both, tails = call(
        functools.partial(hidden_kernel, chips),
        [
            shape((total, 2 * ff), BF16),
            shape((2, 16, width), BF16),
        ],
        (where, *wt_near[1:], *wt_far[1:], down_mat, first, hidden, act, slope),
        2 * total * (feats - 2 * width) * ff,
        "hidden_grad",
        scratch=[VMEM((total, ff), F32)],
    )

    def total_of(*terms):
        return sum(x.astype(F32) for x in terms).astype(BF16)

    keep, send = part(
        where, both, tails, gate_mat, up_mat, width, chips - 1, lambda i: i + 1, chips
    )
    gram_sum, _ = lax.optimization_barrier((gram_sum, wt_near[-1]))
    gram_sum = add(gram_sum, chip_swap(gram_sum, 1))
    send, gram_sum = lax.optimization_barrier((send, gram_sum))
    recv = swap(send)
    through = total_of(keep[1], recv[1])
    long = send.shape[1]
    top, low = hop(through[:mid], 1), hop(through[mid:], chips - 1)
    right = total_of(keep[0], recv[0], jnp.pad(top, ((0, long - mid), (0, 0))))
    left = total_of(keep[2], recv[2], jnp.pad(low, ((mid, 0), (0, 0))))
    keep, send = part(
        where, both, tails, gate_mat, up_mat, width, 1, lambda i: 0, chips, (through,)
    )
    own = total_of(keep[0], swap(send)[0])
    sums = [own, hop(right, 1), hop(left, chips - 1)]
    (payload,) = call(
        final_kernel,
        [shape((total, width + 128), BF16)],
        tuple(sums),
        0,
        "final",
        scalars=0,
        limit=8,
        after=(gram_sum,),
    )
    gram_sum, payload = lax.optimization_barrier((gram_sum, payload))
    gram_sum = add(gram_sum, chip_swap(gram_sum, 2))
    gram_other = swap(gram_sum)
    blocks = feats // BLOCK
    (stats,) = call(
        functools.partial(stats_kernel, chips),
        [shape((blocks, BLOCK // cuts, BLOCK), F32)],
        (where, *wt_near, *wt_far, gram_sum, gram_other),
        4 * total * total * feats // cuts + 2 * total * BLOCK * feats // cuts,
        "stats",
        scratch=[VMEM((total, feats), BF16), VMEM((total, total), BF16)],
        after=(payload,),
    )
    back = exchange(payload.reshape(experts, capacity, width + 128)).reshape(total, width + 128)
    input_grad, logit_grad = call(
        unpack_kernel,
        [shape((tok_rows, width), BF16), shape((1, tok_rows), F32)],
        (slot, logit, back),
        2 * tok_rows * total * (width + 128),
        "unpack",
        scalars=0,
    )
    return input_grad, logit_grad.reshape(tok_rows), stats[None]


def solution(mesh):
    return jax.shard_map(
        shards,
        mesh=mesh,
        in_specs=(
            P("expert", "cuts"),
            P("expert", "cuts"),
            P("expert"),
            P("expert", None),
            P("expert", None, "cuts"),
            P("expert", None, "cuts"),
            P("expert", "cuts", None),
        ),
        out_specs=(P("expert", "cuts"), P("expert"), P("expert", None, "cuts", None)),
        check_vma=False,
    )
```

```python
import functools

import jax
import jax.numpy as jnp
from jax import lax
from jax.experimental import pallas as pl
from jax.experimental.pallas import tpu as pltpu
from jax.sharding import PartitionSpec as P

FF = 4096
BLOCK = 1024
F32 = jnp.float32
BF16 = jnp.bfloat16
VMEM = pltpu.VMEM
LAST = (((1,), (1,)), ((), ()))
FIRST = (((0,), (0,)), ((), ()))


def dot(a, b, dims=(((1,), (0,)), ((), ()))):
    return lax.dot_general(a, b, dims, preferred_element_type=F32)


def iota(shape, dim):
    return lax.broadcasted_iota(jnp.int32, shape, dim)


def whole():
    return pl.BlockSpec(memory_space=VMEM)


def call(body, out, inputs, flops=0, name=None, scratch=(), scalars=1, limit=14, after=(), light=True):
    moved = sum(x.size * x.dtype.itemsize for x in inputs) + sum(
        o.size * o.dtype.itemsize for o in out
    )
    if light:
        flops, moved = 0, 0
    specs = [pl.BlockSpec(memory_space=pltpu.SMEM)] * scalars
    specs += [whole()] * (len(inputs) - scalars)
    specs += [pl.BlockSpec(memory_space=pl.ANY)] * len(after)
    count = len(inputs)

    def kernel(*refs):
        body(*refs[:count], *refs[count + len(after) :])

    return pl.pallas_call(
        kernel,
        out_shape=out,
        in_specs=specs,
        out_specs=[whole()] * len(out),
        scratch_shapes=list(scratch),
        compiler_params=pltpu.CompilerParams(vmem_limit_bytes=limit << 20),
        cost_estimate=pl.CostEstimate(flops=flops, bytes_accessed=moved, transcendentals=0),
        name=name,
    )(*inputs, *after)


def pack_kernel(capacity, cut_ref, ids_ref, tok_ref, tok_out, slot_out):
    ids = ids_ref[...]
    rows = ids.shape[1]
    total = tok_out.shape[0]
    mine = ids == iota((total // capacity, rows), 0)
    earlier = (iota((rows, rows), 0) < iota((rows, rows), 1)).astype(F32).astype(BF16)
    before = dot(mine.astype(F32).astype(BF16), earlier)
    arrival = jnp.sum(jnp.where(mine, before, 0.0), axis=0, keepdims=True)
    slot = ids * capacity + arrival.astype(jnp.int32)
    slot_out[...] = jnp.broadcast_to(slot, slot_out.shape)
    place = (slot == iota((total, rows), 0)).astype(F32).astype(BF16)
    tok_out[...] = dot(place, tok_ref[...]).astype(BF16)


def pack_wt_kernel(slot_ref, wt_ref, wt_out):
    shape = (wt_out.shape[0], slot_ref.shape[1])
    place = (slot_ref[:1] == iota(shape, 0)).astype(F32).astype(BF16)
    wt_out[...] = dot(place, wt_ref[...]).astype(BF16)


def unpack_kernel(slot_ref, logit_ref, back_ref, grad_out, logit_out):
    total = back_ref.shape[0]
    rows, width = grad_out.shape
    slot = jnp.transpose(slot_ref[...])[:, :1]
    place = (slot == iota((rows, total), 1)).astype(F32).astype(BF16)
    own = dot(place, back_ref[...])
    grad_out[...] = own[:, :width].astype(BF16)
    gate_dot = jnp.transpose(own[:, width:])[:1]
    logit_out[...] = (1.0 - jax.nn.sigmoid(logit_ref[...])) * gate_dot


def block_of(cut, hop, other, chips):
    chip = (cut // 2 + chips - hop) % chips
    core = cut % 2
    return 2 * chip + (1 - core if other else core)


def at(index, size):
    return pl.ds(pl.multiple_of(index * size, size), size)


def gates_kernel(chips, cut_ref, *refs):
    near, far = refs[:chips], refs[chips : 2 * chips]
    gate_ref, up_ref, hid_out, act_out, slope_out, send_out, keep_out, gram = refs[2 * chips :]
    cut = cut_ref[0]
    width = near[0].shape[1]
    for ref, out in ((gate_ref, act_out), (up_ref, slope_out)):
        for k in range(chips):
            rows = jnp.concatenate([near[k][...], far[k][...]], axis=1)
            mat = [ref[at(block_of(cut, k, o, chips), width), :] for o in (False, True)]
            mat = jnp.concatenate(mat, axis=0)
            if k == 0:
                out[...] = dot(rows, mat)
            else:
                out[...] += dot(rows, mat)
    gate_pre = act_out[...]
    up_pre = slope_out[...]
    sig = jax.nn.sigmoid(gate_pre)
    act = gate_pre * sig
    hidden = (act * up_pre).astype(BF16)
    act_out[...] = act
    slope_out[...] = up_pre * (sig * (1.0 + gate_pre * (1.0 - sig)))
    hid_out[...] = hidden
    gram[...] = dot(hidden, hidden, LAST)
    half = send_out.shape[0]
    keep_out[...] = gram[at(cut % 2, half), :].astype(BF16)
    send_out[...] = gram[at(1 - cut % 2, half), :].astype(BF16)


def encode(flat, width, base):
    rest = flat.shape[1] - width
    over = jnp.concatenate([flat[:, width:], jnp.zeros((8, width - rest), F32)], axis=1)
    left = jnp.concatenate([flat[:, :width], over], axis=0)
    row = iota(left.shape, 0) % 8 - base
    tail = jnp.zeros_like(left)
    for n in range(2):
        term = left.astype(BF16).astype(F32)
        tail = jnp.where(row == n, term, tail)
        left = left - term
    return tail.astype(BF16)


def decode(tail, total):
    flat = [jnp.sum(tail[8 * n : 8 * n + 8], axis=0, keepdims=True) for n in range(2)]
    return jnp.concatenate([flat[0], flat[1][:, : total - flat[0].shape[1]]], axis=1)


def down_product(down_ref, cut, near, far, hop, chips):
    width = near.shape[1]
    mat = [down_ref[:, at(block_of(cut, hop, o, chips), width)] for o in (False, True)]
    rows = jnp.concatenate([near[...], far[...]], axis=1)
    return dot(rows, jnp.concatenate(mat, axis=1), LAST)


def own_hidden_kernel(chips, cut_ref, near, far, down_ref, out):
    out[...] = down_product(down_ref, cut_ref[0], near, far, 0, chips)


def hidden_kernel(chips, cut_ref, *refs):
    near, far = refs[: chips - 1], refs[chips - 1 : 2 * chips - 2]
    down_ref, first_ref, hid_ref, act_ref, slope_ref = refs[2 * chips - 2 : 2 * chips + 3]
    both_out, tail_out, acc = refs[2 * chips + 3 :]
    cut = cut_ref[0]
    for k in range(1, chips):
        start = first_ref if k == 1 else acc
        acc[...] = start[...] + down_product(down_ref, cut, near[k - 1], far[k - 1], k, chips)
    grad = acc[...]
    ff = grad.shape[1]
    both_out[:, :ff] = (grad * slope_ref[...]).astype(BF16)
    both_out[:, ff:] = (grad * act_ref[...]).astype(BF16)
    dots = jnp.sum(hid_ref[...].astype(F32) * grad, axis=1, keepdims=True)
    flat = jnp.transpose(jnp.broadcast_to(dots, (dots.shape[0], 128)))[:8]
    width = near[0].shape[1]
    tail_out[0] = encode(flat, width, 2 * (cut % 2))
    tail_out[1] = encode(flat, width, 4 + 2 * (cut % 2))


def part_kernel(cut_ref, both_ref, tail_ref, gate_own, gate_oth, up_own, up_oth, *refs):
    keep_out, send_out = refs[-2:]
    gate = jnp.concatenate([gate_own[...], gate_oth[...]], axis=0)
    up = jnp.concatenate([up_own[...], up_oth[...]], axis=0)
    out = dot(both_ref[...], jnp.concatenate([gate, up], axis=1), LAST).astype(BF16)
    total, width = both_ref.shape[0], keep_out.shape[2]
    keep_out[0, :total, :] = out[:, :width]
    send_out[0, :total, :] = out[:, width:]
    keep_out[0, total:, :] = tail_ref[0]
    send_out[0, total:, :] = tail_ref[0]


def part(where, both, tail, gate_mat, up_mat, width, count, hop_of, chips, after=()):
    rows, ff = both.shape[0], gate_mat.shape[1]
    mats = [
        pl.BlockSpec(
            (width, ff), lambda i, w, o=o: (block_of(w[0], chips - hop_of(i), o, chips), 0)
        )
        for o in (False, True, False, True)
    ]
    long = rows + tail.shape[1]
    out = jax.ShapeDtypeStruct((count, long, width), BF16)
    block = pl.BlockSpec((1, long, width), lambda i, w: (i, 0, 0))
    return pl.pallas_call(
        part_kernel,
        out_shape=[out, out],
        grid_spec=pltpu.PrefetchScalarGridSpec(
            num_scalar_prefetch=1,
            grid=(count,),
            in_specs=[
                pl.BlockSpec((rows, 2 * ff), lambda i, w: (0, 0)),
                pl.BlockSpec(
                    (1,) + tail.shape[1:],
                    lambda i, w: (jnp.where(hop_of(i) == chips // 2, 1, 0), 0, 0),
                ),
            ]
            + mats
            + [pl.BlockSpec(memory_space=pl.ANY)] * len(after),
            out_specs=[block, block],
        ),
        compiler_params=pltpu.CompilerParams(vmem_limit_bytes=12 << 20),
        cost_estimate=pl.CostEstimate(
            flops=8 * rows * ff * width * count,
            bytes_accessed=(4 << 20) * count,
            transcendentals=0,
        ),
        name="input_part",
    )(where, both, tail, gate_mat, gate_mat, up_mat, up_mat, *after)


def final_kernel(*refs):
    sums, out = refs[:-1], refs[-1]
    rows = out.shape[0]
    width = sums[0].shape[1]
    total = sums[0][...].astype(F32)
    for ref in sums[1:]:
        total = total + ref[...].astype(F32)
    out[:, :width] = total[:rows].astype(BF16)
    flat = decode(total[rows:], rows)
    lane = jnp.transpose(jnp.broadcast_to(flat, (out.shape[1] - width, rows)))
    out[:, width:] = lane.astype(BF16)


def stats_kernel(chips, cut_ref, *refs):
    near, far = refs[:chips], refs[chips : 2 * chips]
    own_k, oth_k, out, rows, gram = refs[2 * chips :]
    cut = cut_ref[0]
    width = near[0].shape[1]
    for k in range(chips):
        rows[:, at(block_of(cut, k, False, chips), width)] = near[k][...]
        rows[:, at(block_of(cut, k, True, chips), width)] = far[k][...]
    half = own_k.shape[0]
    gram[at(cut % 2, half), :] = own_k[...]
    gram[at(1 - cut % 2, half), :] = oth_k[...]
    share = out.shape[1]
    blocks = out.shape[0]
    per = BLOCK // share
    own = jnp.concatenate([rows[:, at(per * j + cut, share)] for j in range(blocks)], axis=1)
    mixed = dot(gram[...], own).astype(BF16)
    for j in range(blocks):
        out[j] = dot(
            mixed[:, j * share : (j + 1) * share], rows[:, j * BLOCK : (j + 1) * BLOCK], FIRST
        ) * (1.0 / FF)


def shards(tokens, out_grad, gate_logit, expert_ids, w_gate, w_up, w_down):
    experts = lax.axis_size("expert")
    cuts = lax.axis_size("cuts")
    chips = cuts // 2
    tok_rows, width = tokens.shape
    capacity = 2 * tok_rows // experts
    total = experts * capacity
    gate_mat, up_mat, down_mat = w_gate[0], w_up[0], w_down[0]
    ff, feats = down_mat.shape
    shape = jax.ShapeDtypeStruct
    cut = lax.axis_index("cuts").astype(jnp.int32)
    where = cut.reshape(1)

    def hop(x, k):
        if k == 0:
            return x
        return lax.ppermute(
            x, "cuts", [(2 * i + c, 2 * ((i + k) % chips) + c) for i in range(chips) for c in (0, 1)]
        )

    def swap(x):
        return lax.ppermute(x, "cuts", [(i, i ^ 1) for i in range(cuts)])

    def exchange(x):
        return lax.all_to_all(x, "expert", split_axis=0, concat_axis=0, tiled=True)

    ids = expert_ids.reshape(1, tok_rows)
    logit = gate_logit.reshape(1, tok_rows)
    tok_pack, slot = call(
        functools.partial(pack_kernel, capacity),
        [shape((total, width), BF16), shape((8, tok_rows), jnp.int32)],
        (where, ids, tokens),
        0,
        "pack",
        limit=8,
    )
    tok_in = exchange(tok_pack.reshape(experts, capacity, width)).reshape(total, width)
    late_grad, late_logit, tok_in = lax.optimization_barrier((out_grad, gate_logit, tok_in))
    score = jax.nn.sigmoid(late_logit)
    weighted = (score[:, None] * late_grad.astype(F32)).astype(BF16)
    (wt_pack,) = call(
        pack_wt_kernel,
        [shape((total, width), BF16)],
        (slot, weighted),
        0,
        "pack_wt",
        scalars=0,
        limit=8,
    )
    wt_in = exchange(wt_pack.reshape(experts, capacity, width)).reshape(total, width)
    mid = total // 2
    tok_near = [hop(tok_in, k) for k in range(chips)]
    tok_far = [swap(x) for x in tok_near]
    wt_in, _ = lax.optimization_barrier((wt_in, tok_far))
    wt_near = [hop(wt_in, k) for k in range(chips)]
    wt_swap = swap(wt_in)
    half = total // 2
    hidden, act, slope, gram_send, gram_keep = call(
        functools.partial(gates_kernel, chips),
        [
            shape((total, ff), BF16),
            shape((total, ff), F32),
            shape((total, ff), F32),
            shape((half, total), BF16),
            shape((half, total), BF16),
        ],
        (where, *tok_near, *tok_far, gate_mat, up_mat),
        0,
        "gates",
        scratch=[VMEM((total, total), F32)],
        limit=18,
        after=(wt_swap,),
        light=True,
    )
    def add(x, y):
        return (x.astype(F32) + y.astype(F32)).astype(BF16)

    def chip_swap(x, bit):
        return lax.ppermute(
            x, "cuts", [(2 * i + c, 2 * (i ^ bit) + c) for i in range(chips) for c in (0, 1)]
        )

    gram_sum = add(gram_keep, swap(gram_send))
    (first,) = call(
        functools.partial(own_hidden_kernel, chips),
        [shape((total, ff), F32)],
        (where, wt_in, wt_swap, down_mat),
        4 * total * width * ff,
        "own_hidden_grad",
        after=(hidden,),
        light=True,
    )
    wt_far = [wt_swap]
    for k in range(1, chips):
        late, _ = lax.optimization_barrier((wt_near[k], first))
        wt_far.append(swap(late))
    both, tails = call(
        functools.partial(hidden_kernel, chips),
        [
            shape((total, 2 * ff), BF16),
            shape((2, 16, width), BF16),
        ],
        (where, *wt_near[1:], *wt_far[1:], down_mat, first, hidden, act, slope),
        2 * total * (feats - 2 * width) * ff,
        "hidden_grad",
        scratch=[VMEM((total, ff), F32)],
    )

    def total_of(*terms):
        return sum(x.astype(F32) for x in terms).astype(BF16)

    keep, send = part(
        where, both, tails, gate_mat, up_mat, width, chips - 1, lambda i: i + 1, chips
    )
    gram_sum, _ = lax.optimization_barrier((gram_sum, wt_near[-1]))
    gram_sum = add(gram_sum, chip_swap(gram_sum, 1))
    send, gram_sum = lax.optimization_barrier((send, gram_sum))
    recv = swap(send)
    through = total_of(keep[1], recv[1])
    long = send.shape[1]
    top, low = hop(through[:mid], 1), hop(through[mid:], chips - 1)
    right = total_of(keep[0], recv[0], jnp.pad(top, ((0, long - mid), (0, 0))))
    left = total_of(keep[2], recv[2], jnp.pad(low, ((mid, 0), (0, 0))))
    keep, send = part(
        where, both, tails, gate_mat, up_mat, width, 1, lambda i: 0, chips, (through,)
    )
    own = total_of(keep[0], swap(send)[0])
    sums = [own, hop(right, 1), hop(left, chips - 1)]
    (payload,) = call(
        final_kernel,
        [shape((total, width + 128), BF16)],
        tuple(sums),
        0,
        "final",
        scalars=0,
        limit=8,
        after=(gram_sum,),
    )
    gram_sum, payload = lax.optimization_barrier((gram_sum, payload))
    gram_sum = add(gram_sum, chip_swap(gram_sum, 2))
    gram_other = swap(gram_sum)
    blocks = feats // BLOCK
    (stats,) = call(
        functools.partial(stats_kernel, chips),
        [shape((blocks, BLOCK // cuts, BLOCK), F32)],
        (where, *wt_near, *wt_far, gram_sum, gram_other),
        4 * total * total * feats // cuts + 2 * total * BLOCK * feats // cuts,
        "stats",
        scratch=[VMEM((total, feats), BF16), VMEM((total, total), BF16)],
        after=(payload,),
    )
    back = exchange(payload.reshape(experts, capacity, width + 128)).reshape(total, width + 128)
    input_grad, logit_grad = call(
        unpack_kernel,
        [shape((tok_rows, width), BF16), shape((1, tok_rows), F32)],
        (slot, logit, back),
        2 * tok_rows * total * (width + 128),
        "unpack",
        scalars=0,
    )
    return input_grad, logit_grad.reshape(tok_rows), stats[None]


def solution(mesh):
    return jax.shard_map(
        shards,
        mesh=mesh,
        in_specs=(
            P("expert", "cuts"),
            P("expert", "cuts"),
            P("expert"),
            P("expert", None),
            P("expert", None, "cuts"),
            P("expert", None, "cuts"),
            P("expert", "cuts", None),
        ),
        out_specs=(P("expert", "cuts"), P("expert"), P("expert", None, "cuts", None)),
        check_vma=False,
    )
```
